256 devices in a mesh: branch: 16 (over x, z_hi), seq: 16 (over y, z_lo, core).
Axes of the slice: x: 4, y: 4, z: 8 (z_hi: 4, z_lo: 2; z = z_hi * 2 + z_lo), core: 2. Of those that a mesh axis runs over, the one named last changes fastest.
Arguments:
- query_proj: bfloat16 [16, 4096, 3072], P('branch', 'seq'), may hold values from -6 to 6
- key_proj: bfloat16 [16, 4096, 3072], P('branch', 'seq'), may hold values from -6 to 6
- value_proj: bfloat16 [16, 4096, 3072], P('branch', 'seq'), may hold values from -6 to 6
- learn_rate: bfloat16 [16, 4096, 48], P('branch', 'seq'), may hold values from 0.0099487305 to 0.29882812
- norm_gain: float32 [48, 64], P('seq'), may hold values from 0.25 to 1.75
- norm_shift: float32 [48, 64], P('seq'), may hold values from -3 to 3
- start_offset: int32 [16], P('branch'), may hold values from 0 to 4095
- owner_map: int32 [16], replicated, may hold values from 0 to 15, as said below
- first_weight: float32 [16, 48, 64, 256], P('branch', 'seq'), may hold values from -0.75 to 0.75
- first_bias: float32 [16, 48, 256], P('branch', 'seq'), may hold values from -3 to 3
- second_weight: float32 [16, 48, 256, 64], P('branch', 'seq'), may hold values from -0.375 to 0.375
- second_bias: float32 [16, 48, 64], P('branch', 'seq'), may hold values from -3 to 3
Outputs:
- layer_out: bfloat16 [16, 4096, 3072], P('branch', 'seq')
The draws below stay inside these ranges and needn't reach their ends.
Inputs may be any that keep to these rules, and one draw needn't show every extreme that they name: `owner_map`: each entry names a branch.
All inputs are finite; a program needn't handle non-finite values.
Results may differ from the reference program's by a relative error of at most 0.0019.
Values may be sent and summed in bfloat16 or wider, within the bound.
No kernel may reach another device: no remote copies, remote signals or barrier semaphores. Data moves between devices by JAX's collectives and lax.ppermute only.
A program may use at most 128 MiB of HBM per device.

```python
import math
import jax
import jax.numpy as jnp
from jax import lax

H = 48
HEAD = 64
INNER = 256
MB = 64
TOKENS = 4096
BRANCHES = 16
D = 3072


def draw_owner_map(key, part):
    key = jax.random.fold_in(key, 7)
    key_base, key_pick = jax.random.split(key)
    owners = jax.random.randint(key_base, (BRANCHES,), 0, BRANCHES, dtype=jnp.int32)
    first_pick = jax.random.randint(key_pick, (), 0, BRANCHES, dtype=jnp.int32)
    second_pick = (first_pick + BRANCHES // 2) % BRANCHES
    low_pick = (first_pick + 1) % BRANCHES
    high_pick = (first_pick + BRANCHES // 2 + 1) % BRANCHES
    branch_ids = jnp.arange(BRANCHES, dtype=jnp.int32)
    owners = jnp.where(branch_ids == low_pick, jnp.zeros_like(owners), owners)
    owners = jnp.where(branch_ids == high_pick, jnp.full_like(owners, BRANCHES - 1), owners)
    owners = jnp.where(branch_ids == second_pick, (branch_ids - BRANCHES // 2) % BRANCHES, owners)
    owners = jnp.where(branch_ids == first_pick, (branch_ids - 1) % BRANCHES, owners)
    return owners.astype(jnp.int32)


def set_ends(values, key, least, top_value):
    shape = values.shape
    place = [jax.random.randint(jax.random.fold_in(key, axis), (), 0, shape[axis]) for axis in range(len(shape))]
    values = values.at[tuple(place)].set(least)
    longest = shape.index(max(shape))
    place[longest] = (place[longest] + 1) % shape[longest]
    return values.at[tuple(place)].set(top_value)


def block_levels(stream_key, dims, shards, low, top_value):
    level, own = 1.0, jax.random.fold_in(stream_key, 6)
    for axis_at, shards_of in shards:
        steps = jnp.exp(jax.random.uniform(jax.random.fold_in(own, axis_at), (shards_of,), jnp.float32, low / len(shards), top_value / len(shards)))
        level = level * jnp.repeat(steps, dims[axis_at] // shards_of).reshape([-1 if axis == axis_at else 1 for axis in range(len(dims))])
    return level


def gaussian(key, extent, deviation, reach, shards=(), held_as=jnp.bfloat16):
    values = jax.random.normal(key, extent, jnp.float32) * deviation
    if len(shards) > 0:
        values = block_levels(key, extent, shards, -0.22, 0.18) * values
    return jnp.clip(values, min=-reach, max=reach).astype(held_as)


def setup_inputs(seed: int = 0) -> dict:
    key_of = jax.random.split(jax.random.key(seed), 13)
    query_proj = gaussian(key_of[0], (BRANCHES, TOKENS, D), 1.0, 6.0, ((0, 16), (1, 16)))
    key_proj = gaussian(key_of[1], (BRANCHES, TOKENS, D), 1.0, 6.0, ((0, 16), (1, 16)))
    value_proj = gaussian(key_of[2], (BRANCHES, TOKENS, D), 1.0, 6.0, ((0, 16), (1, 16)))
    learn_rate = jnp.clip(jnp.exp(math.log(0.29882812) - 3.4024236 * jax.random.uniform(key_of[3], (BRANCHES, TOKENS, H), jnp.float32) ** block_levels(key_of[3], (BRANCHES, TOKENS, H), ((0, 16), (1, 16)), -0.2, 0.2)), 0.0099487305, 0.29882812).astype(jnp.bfloat16)
    norm_gain = jnp.clip(1.0 + 0.15 * jax.random.normal(key_of[4], (H, HEAD), jnp.float32), 0.25, 1.75)
    norm_shift = gaussian(key_of[5], (H, HEAD), 0.5, 3.0, ((0, 16),), jnp.float32)
    start_offset = set_ends(jax.random.randint(key_of[6], (BRANCHES,), 0, 4096), jax.random.fold_in(key_of[6], 1), 0, 4095).astype(jnp.int32)
    owner_map = draw_owner_map(jax.random.fold_in(key_of[12], 71), 0)
    first_weight = gaussian(key_of[8], (BRANCHES, H, HEAD, INNER), HEAD ** -0.5, 0.75, ((0, 16), (1, 16)), jnp.float32)
    first_bias = gaussian(key_of[9], (BRANCHES, H, INNER), 0.5, 3.0, ((0, 16), (1, 16)), jnp.float32)
    second_weight = gaussian(key_of[10], (BRANCHES, H, INNER, HEAD), INNER ** -0.5, 0.375, ((0, 16), (1, 16)), jnp.float32)
    second_bias = gaussian(key_of[11], (BRANCHES, H, HEAD), 0.5, 3.0, ((0, 16), (1, 16)), jnp.float32)
    return dict(query_proj=query_proj, key_proj=key_proj, value_proj=value_proj, learn_rate=learn_rate, norm_gain=norm_gain, norm_shift=norm_shift, start_offset=start_offset, owner_map=owner_map, first_weight=first_weight, first_bias=first_bias, second_weight=second_weight, second_bias=second_bias)


HIGHEST = lax.Precision.HIGHEST

def rotate(values_in, positions):
    half = values_in.shape[-1] // 2
    freqs = jnp.exp(-jnp.log(10000.0) * jnp.arange(half, dtype=jnp.float32) / half)
    angles = positions.astype(jnp.float32)[:, None] * freqs[None, :]
    cosine = jnp.cos(angles)[:, None, :]
    sine = jnp.sin(angles)[:, None, :]
    first = values_in[..., :half]
    second = values_in[..., half:]
    return jnp.concatenate([first * cosine - second * sine, first * sine + second * cosine], -1)

def norm_out(hidden, gain, shift):
    center = hidden - lax.optimization_barrier(jnp.mean(hidden, -1, keepdims=True))
    spread = lax.optimization_barrier(jnp.mean(center * center, -1, keepdims=True))
    return center * lax.rsqrt(spread + 1e-06) * gain[:, None, :] + shift[:, None, :]

def inner_model(params, inputs, gain, shift):
    weight_one, bias_one, weight_two, bias_two = params
    hidden = jnp.einsum('hbe,hef->hbf', inputs, weight_one, precision=HIGHEST) + bias_one[:, None, :]
    active = jax.nn.gelu(hidden, approximate=True)
    result = jnp.einsum('hbf,hfe->hbe', active, weight_two, precision=HIGHEST) + bias_two[:, None, :]
    return norm_out(result, gain, shift)

def inner_loss(params, inputs, target, rates, gain, shift):
    error = inner_model(params, inputs, gain, shift) - target
    return 0.5 * jnp.sum(rates[..., None] * error * error) / inputs.shape[1]

def inner_step(params, block, gain, shift):
    query, keyed, valued, rates = block
    grads = jax.grad(inner_loss)(params, keyed, valued - keyed, rates, gain, shift)
    params = tuple((param - grad for param, grad in zip(params, grads)))
    return (params, query + inner_model(params, query, gain, shift))

def run_heads(params, query, keyed, valued, rates, gain, shift, block_len):
    blocks = query.shape[1] // block_len

    def split_blocks(array):
        shaped = array.reshape((array.shape[0], blocks, block_len) + array.shape[2:])
        return jnp.moveaxis(shaped, 1, 0)

    def advance(carry, block):
        return inner_step(carry, block, gain, shift)
    params, results = lax.scan(advance, params, (split_blocks(query), split_blocks(keyed), split_blocks(valued), split_blocks(rates)), unroll=4)
    results = jnp.moveaxis(results, 0, 1)
    return results.reshape(query.shape)

def reference(query_proj, key_proj, value_proj, learn_rate, norm_gain, norm_shift, start_offset, owner_map, first_weight, first_bias, second_weight, second_bias):

    def one_branch(which):
        source = owner_map[which]
        params = (first_weight[source], first_bias[source], second_weight[source], second_bias[source])
        positions = start_offset[which] + jnp.arange(TOKENS, dtype=jnp.int32)
        query = rotate(query_proj[which].astype(jnp.float32).reshape(TOKENS, H, HEAD), positions)
        keyed = rotate(key_proj[which].astype(jnp.float32).reshape(TOKENS, H, HEAD), positions)
        valued = value_proj[which].astype(jnp.float32).reshape(TOKENS, H, HEAD)
        rates = jnp.swapaxes(learn_rate[which].astype(jnp.float32), 0, 1)
        result = run_heads(params, jnp.swapaxes(query, 0, 1), jnp.swapaxes(keyed, 0, 1), jnp.swapaxes(valued, 0, 1), rates, norm_gain, norm_shift, MB)
        return jnp.swapaxes(result, 0, 1).reshape(TOKENS, H * HEAD).astype(jnp.bfloat16)
    return lax.map(one_branch, jnp.arange(BRANCHES, dtype=jnp.int32))
```

```python
import jax
import jax.numpy as jnp
from jax import lax
from jax.experimental import pallas as pl
from jax.experimental.pallas import tpu as pltpu
from jax.sharding import PartitionSpec as P

f32, bf16 = jnp.float32, jnp.bfloat16
C0 = 0.7978845608028654
C1 = 0.044715
MB = 64


def split(x):
    hi = x.astype(bf16)
    return hi, (x - hi.astype(f32)).astype(bf16)


def stack4(hi, lo, axis):
    return jnp.concatenate([hi, lo, hi, lo], axis)


def dot(a, b):
    return jnp.dot(a, b, preferred_element_type=f32)


def dot_nt(a, b):
    return lax.dot_general(a, b, (((1,), (1,)), ((), ())), preferred_element_type=f32)


def ttt_kernel(x_ref, cos_ref, sin_ref, gain_ref, shift_ref,
               w1_in, c1_in, w2_in, c2_in, out_ref,
               w1_ref, c1_ref, w2_ref, c2_ref, qprev_ref, yprev_ref):
    nh = w1_ref.shape[0]
    nb = x_ref.shape[0]
    rows = nh * 64
    w1_ref[...] = w1_in[...]
    c1_ref[...] = c1_in[...]
    w2_ref[...] = w2_in[...]
    c2_ref[...] = c2_in[...]
    qprev_ref[...] = jnp.zeros_like(qprev_ref)
    yprev_ref[...] = jnp.zeros_like(yprev_ref)
    low = lax.broadcasted_iota(jnp.int32, (64, 128), 1) < 64
    low1 = lax.broadcasted_iota(jnp.int32, (1, 128), 1) < 64

    heads = range(nh)

    def tokmajor(x):
        xt = jnp.transpose(jnp.concatenate([x, x], 0))
        hi, lo = split(xt)
        return hi, lo

    def forward(xps):
        xs = [jnp.concatenate(tokmajor(x), 1) for x in xps]
        w1s = [stack4(*split(w1_ref[h]), 0) for h in heads]
        hid = [dot(xs[h], w1s[h]) + c1_ref[h] for h in heads]
        h2 = [x * x for x in hid]
        th = [jnp.tanh(hid[h] * (h2[h] * (C0 * C1) + C0)) for h in heads]
        hh = [0.5 * x for x in hid]
        aa = [split(hh[h] * th[h] + hh[h]) for h in heads]
        ww = [split(w2_ref[h]) for h in heads]
        z4 = [dot_nt(jnp.concatenate(ww[h], 0), jnp.concatenate(aa[h], 0)) for h in heads]
        z = [(z[:64, :128] + z[64:, 128:]) + (z[64:, :128] + z[:64, 128:]) + c2_ref[h] for h, z in enumerate(z4)]
        c = [z[h] - jnp.mean(z[h], 0, keepdims=True) for h in heads]
        rstd = [lax.rsqrt(jnp.mean(c[h] * c[h], 0, keepdims=True) + 1e-06) for h in heads]
        return hid, h2, th, hh, aa, ww, c, rstd

    def step(xp, pq, bc, rate, xdup, even):
        hid, h2, th, hh, aa, ww, c, rstd = forward(xp)
        lo_k = 0 if even else 64
        sl = slice(lo_k, lo_k + 64)
        dz, y = [], []
        for h in heads:
            gain = gain_ref[h]
            y.append(c[h] * rstd[h] * gain + pq[h])
            g2c = gain * gain * c[h]
            m2 = jnp.mean(g2c, 0, keepdims=True)
            m3 = jnp.mean(g2c * c[h], 0, keepdims=True)
            m4 = jnp.mean(bc[h] * c[h], 0, keepdims=True)
            s = rstd[h] * rate[h]
            e = rstd[h] * rstd[h] * (rstd[h] * m3 + m4)
            dz.append(s * ((g2c - m2) * rstd[h] + bc[h] - c[h] * e))
        lhs = []
        for h in heads:
            dzh, dzl = tokmajor(dz[h])
            lhs.append(jnp.concatenate([dzh[sl], dzl[sl]], 1))
        da = [dot(lhs[h], stack4(*ww[h], 0)) for h in heads]
        gp = []
        for h in heads:
            hk, h2k, thk, hhk = hid[h][sl], h2[h][sl], th[h][sl], hh[h][sl]
            du = h2k * (3 * C0 * C1) + C0
            gp.append((0.5 * thk + 0.5) + (hhk * du) * (1.0 - thk * thk))
        dh = [da[h] * gp[h] for h in heads]
        dw1 = [dot(xdup[h], stack4(*split(dh[h]), 0)) for h in heads]
        dw2 = []
        for h in heads:
            d = dz[h] + pltpu.roll(dz[h], 64, 1)
            dw2.append(dot(jnp.concatenate(split(d), 1), stack4(aa[h][0][sl], aa[h][1][sl], 0)))
        for h in heads:
            w2_ref[h] = w2_ref[h] - dw2[h]
            c2_ref[h] = c2_ref[h] - jnp.sum(dz[h], 1, keepdims=True)
            w1_ref[h] = w1_ref[h] - dw1[h]
            c1_ref[h] = c1_ref[h] - jnp.sum(dh[h], 0, keepdims=True)
        return y

    def rot(x, cs, sn):
        a, b = x[:32], x[32:]
        return jnp.concatenate([a * cs - b * sn, a * sn + b * cs], 0)

    def block(b, _):
        for tile in range(2):
            ts = slice(tile * 128, tile * 128 + 128)
            cs = cos_ref[b, :, ts]
            sn = sin_ref[b, :, ts]
            ks, qs, ps, bcs, rts, xds = [], [], [], [], [], []
            rates = x_ref[b, 3 * rows:3 * rows + 16, ts].astype(f32) * (1.0 / MB)
            for h in heads:
                q = rot(x_ref[b, h * 64:h * 64 + 64, ts].astype(f32), cs, sn)
                k = rot(x_ref[b, rows + h * 64:rows + h * 64 + 64, ts].astype(f32), cs, sn)
                v = x_ref[b, 2 * rows + h * 64:2 * rows + h * 64 + 64, ts].astype(f32)
                bb = gain_ref[h] * (shift_ref[h] - (v - k))
                bc = bb - jnp.mean(bb, 0, keepdims=True)
                kr = pltpu.roll(k, 64, 1)
                ks.append(k)
                qs.append(q)
                bcs.append(bc)
                rts.append(rates[h:h + 1])
                e_hi, e_lo = split(jnp.where(low, k, kr))
                o_hi, o_lo = split(jnp.where(low, kr, k))
                xds.append((jnp.concatenate([e_hi, e_lo], 1), jnp.concatenate([o_hi, o_lo], 1)))
            pb = jnp.maximum(b - 1, 0) if tile == 0 else b
            pts = slice(128, 256) if tile == 0 else slice(0, 128)
            qp = [qprev_ref[h] for h in heads]
            y = step([jnp.where(low, ks[h], qp[h]) for h in heads], [qp[h] + shift_ref[h] for h in heads], bcs,
                     [jnp.where(low1, rts[h], 0.0) for h in heads], [x[0] for x in xds], True)
            for h in heads:
                hs = slice(h * 64, h * 64 + 64)
                out_ref[pb, hs, pts] = jnp.where(low, yprev_ref[h], y[h]).astype(bf16)
            y = step([jnp.where(low, qs[h], ks[h]) for h in heads], [qs[h] + shift_ref[h] for h in heads], bcs,
                     [jnp.where(low1, 0.0, rts[h]) for h in heads], [x[1] for x in xds], False)
            for h in heads:
                yprev_ref[h] = y[h]
                qprev_ref[h] = qs[h]
        return 0

    lax.fori_loop(0, nb, block, 0)
    qp = [qprev_ref[h] for h in heads]
    c, rstd = forward(qp)[-2:]
    for h in heads:
        hs = slice(h * 64, h * 64 + 64)
        y = c[h] * rstd[h] * gain_ref[h] + qp[h] + shift_ref[h]
        out_ref[nb - 1, hs, 128:256] = jnp.where(low, yprev_ref[h], y).astype(bf16)


def ttt(x, cos, sin, gain, shift, w1, c1, w2, c2):
    nh = w1.shape[0]
    return pl.pallas_call(
        ttt_kernel,
        out_shape=jax.ShapeDtypeStruct((x.shape[0], nh * 64, x.shape[2]), bf16),
        in_specs=[pl.BlockSpec(memory_space=pltpu.VMEM)] * 9,
        out_specs=pl.BlockSpec(memory_space=pltpu.VMEM),
        scratch_shapes=[
            pltpu.VMEM((nh, 64, 256), f32),
            pltpu.VMEM((nh, 1, 256), f32),
            pltpu.VMEM((nh, 64, 256), f32),
            pltpu.VMEM((nh, 64, 128), f32),
            pltpu.VMEM((nh, 64, 128), f32),
            pltpu.VMEM((nh, 64, 128), f32),
        ],
        compiler_params=pltpu.CompilerParams(vmem_limit_bytes=48 * 1024 * 1024),
    )(x, cos, sin, gain, shift, w1, c1, w2, c2)


def tables(off, n):
    half = 32
    freqs = jnp.exp(-jnp.log(10000.0) * jnp.arange(half, dtype=f32) / half)
    pos = (off + jnp.arange(n, dtype=jnp.int32)).astype(f32)
    ang = pos.reshape(n // 256, 1, 256) * freqs[None, :, None]
    return jnp.cos(ang), jnp.sin(ang)


def body(
    query_proj,
    key_proj,
    value_proj,
    learn_rate,
    norm_gain,
    norm_shift,
    start_offset,
    owner_map,
    first_weight,
    first_bias,
    second_weight,
    second_bias,
):
    groups = lax.axis_size("seq")
    nh, tok = first_weight.shape[1], query_proj.shape[1]
    source = owner_map[lax.axis_index("branch")]

    w2t = jnp.swapaxes(second_weight[0], 1, 2)
    packed = jnp.concatenate([first_weight[0], w2t], 0).reshape(16, 24, 256)
    held = lax.all_to_all(packed, "branch", split_axis=0, concat_axis=0, tiled=True)
    picked = jnp.take(held, owner_map, axis=0)
    own = lax.all_to_all(picked, "branch", split_axis=0, concat_axis=0, tiled=True)
    own = own.reshape(2 * nh, 64, 256)
    biases = lax.all_gather(jnp.concatenate([first_bias[0], second_bias[0]], 1), "branch")
    bias = lax.dynamic_index_in_dim(biases, source, 0, keepdims=False)
    w1, w2 = own[:nh], own[nh:]
    w2 = w2 - jnp.mean(w2, 1, keepdims=True)
    c1, c2 = bias[:, :256], bias[:, 256:]
    c2 = c2 - jnp.mean(c2, 1, keepdims=True)

    def column(x):
        return jnp.broadcast_to(x[:, :, None], x.shape + (128,))

    def by_group(x):
        return x[0].T.reshape(groups, x.shape[2] // groups, tok)

    rates = jnp.pad(by_group(learn_rate), ((0, 0), (0, 16 - nh), (0, 0)))
    x = jnp.concatenate([by_group(query_proj), by_group(key_proj), by_group(value_proj), rates], 1)
    x = lax.all_to_all(x, "seq", split_axis=0, concat_axis=0, tiled=True)
    cos, sin = tables(start_offset[0], groups * tok)
    y = ttt(x, cos, sin, column(norm_gain), column(norm_shift), w1, c1[:, None, :], w2, column(c2))
    y = lax.all_to_all(y, "seq", split_axis=0, concat_axis=0, tiled=True)
    return y.reshape(groups * nh * 64, tok).T[None]


def solution(mesh):
    return jax.shard_map(
        body,
        mesh=mesh,
        in_specs=(
            P("branch", "seq", None),
            P("branch", "seq", None),
            P("branch", "seq", None),
            P("branch", "seq", None),
            P("seq", None),
            P("seq", None),
            P("branch"),
            P(),
            P("branch", "seq", None, None),
            P("branch", "seq", None),
            P("branch", "seq", None, None),
            P("branch", "seq", None),
        ),
        out_specs=P("branch", "seq", None),
        check_vma=False,
    )
```

```python
import jax
import jax.numpy as jnp
from jax import lax
from jax.experimental import pallas as pl
from jax.experimental.pallas import tpu as pltpu
from jax.sharding import PartitionSpec as P

f32, bf16 = jnp.float32, jnp.bfloat16
C0 = 0.7978845608028654
C1 = 0.044715
MB = 64


def split(x):
    hi = x.astype(bf16)
    return hi, (x - hi.astype(f32)).astype(bf16)


def stack4(hi, lo, axis):
    return jnp.concatenate([hi, lo, hi, lo], axis)


def dot(a, b):
    return jnp.dot(a, b, preferred_element_type=f32)


def dot_nt(a, b):
    return lax.dot_general(a, b, (((1,), (1,)), ((), ())), preferred_element_type=f32)


def ttt_kernel(x_ref, cos_ref, sin_ref, gain_ref, shift_ref,
               own_ref, out_ref,
               w1_ref, c1_ref, w2_ref, c2_ref, qprev_ref, yprev_ref):
    nh = w1_ref.shape[0]
    heads = range(nh)
    nb = x_ref.shape[0]
    rows = nh * 64
    for h in heads:
        hl = slice(h * 256, h * 256 + 256)
        for i in range(8):
            w1_ref[h, i * 8:i * 8 + 8] = own_ref[i, :, hl]
        w2 = jnp.concatenate([own_ref[8 + i, :, hl] for i in range(8)], 0)
        w2_ref[h] = w2 - jnp.mean(w2, 0, keepdims=True)
        bias = own_ref[0, :, nh * 256:nh * 256 + 128]
        c1_ref[h] = jnp.concatenate([bias[h:h + 1], bias[nh + h:nh + h + 1]], 1)
        c2 = bias[2 * nh + h // 2:2 * nh + h // 2 + 1, h % 2 * 64:h % 2 * 64 + 64]
        c2_ref[h] = jnp.transpose(jnp.broadcast_to(c2 - jnp.mean(c2), (128, 64)))
    qprev_ref[...] = jnp.zeros_like(qprev_ref)
    yprev_ref[...] = jnp.zeros_like(yprev_ref)
    low = lax.broadcasted_iota(jnp.int32, (64, 128), 1) < 64
    low1 = lax.broadcasted_iota(jnp.int32, (1, 128), 1) < 64

    def tokmajor(x):
        xt = jnp.transpose(jnp.concatenate([x, x], 0))
        hi, lo = split(xt)
        return hi, lo

    def forward(xps):
        xs = [jnp.concatenate(tokmajor(x), 1) for x in xps]
        w1s = [stack4(*split(w1_ref[h]), 0) for h in heads]
        hid = [dot(xs[h], w1s[h]) + c1_ref[h] for h in heads]
        h2 = [x * x for x in hid]
        th = [jnp.tanh(hid[h] * (h2[h] * (C0 * C1) + C0)) for h in heads]
        hh = [0.5 * x for x in hid]
        aa = [split(hh[h] * th[h] + hh[h]) for h in heads]
        ww = [split(w2_ref[h]) for h in heads]
        z4 = [dot_nt(jnp.concatenate(ww[h], 0), jnp.concatenate(aa[h], 0)) for h in heads]
        z = [(z[:64, :128] + z[64:, 128:]) + (z[64:, :128] + z[:64, 128:]) + c2_ref[h] for h, z in enumerate(z4)]
        c = [z[h] - jnp.mean(z[h], 0, keepdims=True) for h in heads]
        rstd = [lax.rsqrt(jnp.mean(c[h] * c[h], 0, keepdims=True) + 1e-06) for h in heads]
        return hid, h2, th, hh, aa, ww, c, rstd

    def step(xp, pq, bc, rate, xdup, even):
        hid, h2, th, hh, aa, ww, c, rstd = forward(xp)
        lo_k = 0 if even else 64
        sl = slice(lo_k, lo_k + 64)
        dz, y = [], []
        for h in heads:
            gain = gain_ref[h]
            y.append(c[h] * rstd[h] * gain + pq[h])
            g2c = gain * gain * c[h]
            m2 = jnp.mean(g2c, 0, keepdims=True)
            m3 = jnp.mean(g2c * c[h], 0, keepdims=True)
            m4 = jnp.mean(bc[h] * c[h], 0, keepdims=True)
            s = rstd[h] * rate[h]
            e = rstd[h] * rstd[h] * (rstd[h] * m3 + m4)
            dz.append(s * ((g2c - m2) * rstd[h] + bc[h] - c[h] * e))
        lhs = []
        for h in heads:
            dzh, dzl = tokmajor(dz[h])
            lhs.append(jnp.concatenate([dzh[sl], dzl[sl]], 1))
        da = [dot(lhs[h], stack4(*ww[h], 0)) for h in heads]
        gp = []
        for h in heads:
            hk, h2k, thk, hhk = hid[h][sl], h2[h][sl], th[h][sl], hh[h][sl]
            du = h2k * (3 * C0 * C1) + C0
            gp.append((0.5 * thk + 0.5) + (hhk * du) * (1.0 - thk * thk))
        dh = [da[h] * gp[h] for h in heads]
        dw1 = [dot(xdup[h], stack4(*split(dh[h]), 0)) for h in heads]
        dw2 = []
        for h in heads:
            d = dz[h] + pltpu.roll(dz[h], 64, 1)
            dw2.append(dot(jnp.concatenate(split(d), 1), stack4(aa[h][0][sl], aa[h][1][sl], 0)))
        for h in heads:
            w2_ref[h] = w2_ref[h] - dw2[h]
            c2_ref[h] = c2_ref[h] - jnp.sum(dz[h], 1, keepdims=True)
            w1_ref[h] = w1_ref[h] - dw1[h]
            c1_ref[h] = c1_ref[h] - jnp.sum(dh[h], 0, keepdims=True)
        return y

    def rot(x, cs, sn):
        a, b = x[:32], x[32:]
        return jnp.concatenate([a * cs - b * sn, a * sn + b * cs], 0)

    def block(b, _):
        for tile in range(2):
            ts = slice(tile * 128, tile * 128 + 128)
            cs = cos_ref[b, :, ts]
            sn = sin_ref[b, :, ts]
            ks, qs, ps, bcs, rts, xds = [], [], [], [], [], []
            rates = x_ref[b, 3 * rows:3 * rows + 16, ts].astype(f32) * (1.0 / MB)
            for h in heads:
                q = rot(x_ref[b, h * 64:h * 64 + 64, ts].astype(f32), cs, sn)
                k = rot(x_ref[b, rows + h * 64:rows + h * 64 + 64, ts].astype(f32), cs, sn)
                v = x_ref[b, 2 * rows + h * 64:2 * rows + h * 64 + 64, ts].astype(f32)
                bb = gain_ref[h] * (shift_ref[h] - (v - k))
                bc = bb - jnp.mean(bb, 0, keepdims=True)
                kr = pltpu.roll(k, 64, 1)
                ks.append(k)
                qs.append(q)
                bcs.append(bc)
                rts.append(rates[h:h + 1])
                e_hi, e_lo = split(jnp.where(low, k, kr))
                o_hi, o_lo = split(jnp.where(low, kr, k))
                xds.append((jnp.concatenate([e_hi, e_lo], 1), jnp.concatenate([o_hi, o_lo], 1)))
            pb = jnp.maximum(b - 1, 0) if tile == 0 else b
            pts = slice(128, 256) if tile == 0 else slice(0, 128)
            qp = [qprev_ref[h] for h in heads]
            y = step([jnp.where(low, ks[h], qp[h]) for h in heads], [qp[h] + shift_ref[h] for h in heads], bcs,
                     [jnp.where(low1, rts[h], 0.0) for h in heads], [x[0] for x in xds], True)
            for h in heads:
                hs = slice(h * 64, h * 64 + 64)
                out_ref[pb, hs, pts] = jnp.where(low, yprev_ref[h], y[h]).astype(bf16)
            y = step([jnp.where(low, qs[h], ks[h]) for h in heads], [qs[h] + shift_ref[h] for h in heads], bcs,
                     [jnp.where(low1, 0.0, rts[h]) for h in heads], [x[1] for x in xds], False)
            for h in heads:
                yprev_ref[h] = y[h]
                qprev_ref[h] = qs[h]
        return 0

    lax.fori_loop(0, nb, block, 0)
    qp = [qprev_ref[h] for h in heads]
    c, rstd = forward(qp)[-2:]
    for h in heads:
        hs = slice(h * 64, h * 64 + 64)
        y = c[h] * rstd[h] * gain_ref[h] + qp[h] + shift_ref[h]
        out_ref[nb - 1, hs, 128:256] = jnp.where(low, yprev_ref[h], y).astype(bf16)


def ttt(x, cos, sin, gain, shift, own):
    nh = gain.shape[0]
    return pl.pallas_call(
        ttt_kernel,
        out_shape=jax.ShapeDtypeStruct((x.shape[0], nh * 64, x.shape[2]), bf16),
        in_specs=[pl.BlockSpec(memory_space=pltpu.VMEM)] * 6,
        out_specs=pl.BlockSpec(memory_space=pltpu.VMEM),
        scratch_shapes=[
            pltpu.VMEM((nh, 64, 256), f32),
            pltpu.VMEM((nh, 1, 256), f32),
            pltpu.VMEM((nh, 64, 256), f32),
            pltpu.VMEM((nh, 64, 128), f32),
            pltpu.VMEM((nh, 64, 128), f32),
            pltpu.VMEM((nh, 64, 128), f32),
        ],
        compiler_params=pltpu.CompilerParams(vmem_limit_bytes=48 * 1024 * 1024),
    )(x, cos, sin, gain, shift, own)


def tables(off, n):
    half = 32
    freqs = jnp.exp(-jnp.log(10000.0) * jnp.arange(half, dtype=f32) / half)
    pos = (off + jnp.arange(n, dtype=jnp.int32)).astype(f32)
    ang = pos.reshape(n // 256, 1, 256) * freqs[None, :, None]
    return jnp.cos(ang), jnp.sin(ang)


def body(
    query_proj,
    key_proj,
    value_proj,
    learn_rate,
    norm_gain,
    norm_shift,
    start_offset,
    owner_map,
    first_weight,
    first_bias,
    second_weight,
    second_bias,
):
    groups = lax.axis_size("seq")
    nh, tok = first_weight.shape[1], query_proj.shape[1]

    weights = jnp.stack([first_weight[0], jnp.swapaxes(second_weight[0], 1, 2)])
    weights = weights.reshape(2, nh, 8, 8, 256).transpose(0, 2, 3, 1, 4).reshape(16, 8, nh * 256)
    biases = jnp.concatenate([first_bias[0, :, :128], first_bias[0, :, 128:], jnp.pad(second_bias[0].reshape(1, nh * 64), ((0, 0), (0, 64))).reshape(2, 128)], 0)
    packed = jnp.concatenate([weights, jnp.broadcast_to(biases, (16, 8, 128))], 2)
    held = lax.all_to_all(packed, "branch", split_axis=0, concat_axis=0, tiled=True)
    picked = jnp.take(held, owner_map, axis=0)
    own = lax.all_to_all(picked, "branch", split_axis=0, concat_axis=0, tiled=True)

    def column(x):
        return jnp.broadcast_to(x[:, :, None], x.shape + (128,))

    def by_group(x):
        return x[0].T.reshape(groups, x.shape[2] // groups, tok)

    rates = jnp.pad(by_group(learn_rate), ((0, 0), (0, 16 - nh), (0, 0)))
    x = jnp.concatenate([by_group(query_proj), by_group(key_proj), by_group(value_proj), rates], 1)
    x = lax.all_to_all(x, "seq", split_axis=0, concat_axis=0, tiled=True)
    cos, sin = tables(start_offset[0], groups * tok)
    y = ttt(x, cos, sin, column(norm_gain), column(norm_shift), own)
    y = lax.all_to_all(y, "seq", split_axis=0, concat_axis=0, tiled=True)
    return y.reshape(groups * nh * 64, tok).T[None]


def solution(mesh):
    return jax.shard_map(
        body,
        mesh=mesh,
        in_specs=(
            P("branch", "seq", None),
            P("branch", "seq", None),
            P("branch", "seq", None),
            P("branch", "seq", None),
            P("seq", None),
            P("seq", None),
            P("branch"),
            P(),
            P("branch", "seq", None, None),
            P("branch", "seq", None),
            P("branch", "seq", None, None),
            P("branch", "seq", None),
        ),
        out_specs=P("branch", "seq", None),
        check_vma=False,
    )
```

```python
import jax
import jax.numpy as jnp
from jax import lax
from jax.experimental import pallas as pl
from jax.experimental.pallas import tpu as pltpu
from jax.sharding import PartitionSpec as P

f32, bf16 = jnp.float32, jnp.bfloat16
C0 = 0.7978845608028654
C1 = 0.044715
MB = 64


def split(x):
    hi = x.astype(bf16)
    return hi, (x - hi.astype(f32)).astype(bf16)


def stack4(hi, lo, axis):
    return jnp.concatenate([hi, lo, hi, lo], axis)


def dot(a, b):
    return jnp.dot(a, b, preferred_element_type=f32)


def dot_nt(a, b):
    return lax.dot_general(a, b, (((1,), (1,)), ((), ())), preferred_element_type=f32)


def ttt_kernel(x_ref, cos_ref, sin_ref, gain_ref, shift_ref, own_ref, out_ref,
               w1_ref, c1_ref, w2_ref, c2_ref, yprev_ref, base_ref, corr_ref, dh_ref,
               xk_ref, xq_ref, xt_ref, xd_ref, rate_ref):
    nh = w1_ref.shape[0]
    heads = range(nh)
    nb = x_ref.shape[0]
    rows = nh * 64
    for h in heads:
        hl = slice(h * 256, h * 256 + 256)
        for i in range(8):
            w1_ref[h, i * 8:i * 8 + 8] = own_ref[i, :, hl]
        w2 = jnp.concatenate([own_ref[8 + i, :, hl] for i in range(8)], 0)
        w2_ref[h] = 0.5 * (w2 - jnp.mean(w2, 0, keepdims=True))
        bias = own_ref[0, :, nh * 256:nh * 256 + 128]
        c1_ref[h] = jnp.concatenate([bias[h:h + 1], bias[nh + h:nh + h + 1]], 1)
        c2 = bias[2 * nh + h // 2:2 * nh + h // 2 + 1, h % 2 * 64:h % 2 * 64 + 64]
        c2_ref[h] = jnp.transpose(jnp.broadcast_to(c2 - jnp.mean(c2), (128, 64)))
    yprev_ref[...] = jnp.zeros_like(yprev_ref)
    dh_ref[...] = jnp.zeros_like(dh_ref)
    corr_ref[...] = jnp.zeros_like(corr_ref)
    low = lax.broadcasted_iota(jnp.int32, (64, 128), 1) < 64
    low1 = lax.broadcasted_iota(jnp.int32, (1, 128), 1) < 64

    def tokmajor(x):
        return split(jnp.transpose(jnp.concatenate([x, x], 0)))

    def rot(x, cs, sn):
        a, b = x[:32], x[32:]
        return jnp.concatenate([a * cs - b * sn, a * sn + b * cs], 0)

    def prep(b, tile):
        ts = slice(tile * 128, tile * 128 + 128)
        cs, sn = cos_ref[b, :, ts], sin_ref[b, :, ts]
        rates = x_ref[b, 3 * rows:3 * rows + 16, ts].astype(f32) * (1.0 / MB)
        out = []
        for h in heads:
            q = rot(x_ref[b, h * 64:h * 64 + 64, ts].astype(f32), cs, sn)
            k = rot(x_ref[b, rows + h * 64:rows + h * 64 + 64, ts].astype(f32), cs, sn)
            v = x_ref[b, 2 * rows + h * 64:2 * rows + h * 64 + 64, ts].astype(f32)
            target = gain_ref[h] * (shift_ref[h] - (v - k))
            target = target - jnp.mean(target, 0, keepdims=True)
            kr = pltpu.roll(k, 64, 1)
            even = jnp.concatenate(split(jnp.where(low, k, kr)), 1)
            odd = jnp.concatenate(split(jnp.where(low, kr, k)), 1)
            out.append((k, q, target, even, odd, rates[h:h + 1]))
        return tuple(list(x) for x in zip(*out))

    def normed(z):
        c = z - jnp.mean(z, 0, keepdims=True)
        return c, lax.rsqrt(jnp.mean(c * c, 0, keepdims=True) + 1e-06)

    def hidden(xds):
        upd = [dot(jnp.concatenate([corr_ref[h], xds[h]], 0), stack4(dh_ref[h, :64], dh_ref[h, 64:], 0)) for h in heads]
        return [base_ref[h] - upd[h][:128] for h in heads], [u[128:] for u in upd]

    def gelu(hid, sl):
        act, slope = [], []
        for x in hid:
            sq = x * x
            th = jnp.tanh(x * (sq * (C0 * C1) + C0))
            act.append(split(x * th + x))
            if sl is not None:
                t, v = th[sl], x[sl]
                slope.append((1.0 + t) * ((v * (sq[sl] * (3 * C0 * C1) + C0)) * (1.0 - t) + 1.0))
        return act, slope

    def second(aa, ww):
        z4 = [dot_nt(jnp.concatenate(ww[h], 0), jnp.concatenate(aa[h], 0)) for h in heads]
        return [(z[:64, :128] + z[64:, 128:]) + (z[64:, :128] + z[:64, 128:]) + c2_ref[h] for h, z in enumerate(z4)]

    def ahead(xs, xds, w1, c1):
        for h in heads:
            base_ref[h] = dot(xs[h], stack4(*split(w1[h]), 0)) + c1[h]
        for h in heads:
            hi, lo = xds[h][:, :128], xds[h][:, 128:]
            corr_ref[h] = jnp.concatenate(split(dot(xs[h], stack4(hi, lo, 0)) + 1.0), 1)

    def step(pq, target, rate, xprev, xds, xnext, even):
        sl = slice(0, 64) if even else slice(64, 128)
        hid, dw1 = hidden(xprev)
        aa, gp = gelu(hid, sl)
        w1 = [w1_ref[h] - dw1[h] for h in heads]
        c1 = [c1_ref[h] for h in heads]
        ww = [split(w2_ref[h]) for h in heads]
        z = second(aa, ww)
        ahead([jnp.concatenate(tokmajor(x), 1) for x in xnext], xds, w1, c1)
        dz, y = [], []
        for h in heads:
            c, rstd = normed(z[h])
            gain = gain_ref[h]
            y.append(c * rstd * gain + pq[h])
            g2c = gain * gain * c
            m2 = jnp.mean(g2c, 0, keepdims=True)
            m3 = jnp.mean(g2c * c, 0, keepdims=True)
            m4 = jnp.mean(target[h] * c, 0, keepdims=True)
            s = rstd * rate[h]
            e = rstd * rstd * (rstd * m3 + m4)
            dz.append(s * ((g2c - m2) * rstd + target[h] - c * e))
        lhs = []
        for h in heads:
            dzh, dzl = tokmajor(dz[h])
            lhs.append(jnp.concatenate([dzh[sl], dzl[sl]], 1))
        da = [dot(lhs[h], stack4(*ww[h], 0)) for h in heads]
        dh = [da[h] * gp[h] for h in heads]
        for h in heads:
            dh_ref[h] = jnp.concatenate(split(dh[h]), 0)
        dw2 = []
        for h in heads:
            d = dz[h] + pltpu.roll(dz[h], 64, 1)
            dw2.append(dot(jnp.concatenate(split(d), 1), stack4(aa[h][0][sl], aa[h][1][sl], 0)))
        for h in heads:
            w2_ref[h] = w2_ref[h] - 0.25 * dw2[h]
            c2_ref[h] = c2_ref[h] - jnp.sum(dz[h], 1, keepdims=True)
            w1_ref[h] = w1[h]
            c1_ref[h] = c1[h] - jnp.sum(dh[h], 0, keepdims=True)
        return y

    def tile_steps(cur, nxt, qp, xp):
        k, q, target, even, odd, rate = cur
        ye = step([qp[h] + shift_ref[h] for h in heads], target, [jnp.where(low1, r, 0.0) for r in rate],
                  xp, even, [jnp.where(low, q[h], k[h]) for h in heads], True)
        yo = step([q[h] + shift_ref[h] for h in heads], target, [jnp.where(low1, 0.0, r) for r in rate],
                  even, odd, [jnp.where(low, nxt[0][h], q[h]) for h in heads], False)
        return ye, yo

    def put(b, tile, first, then):
        for h in heads:
            out_ref[b, h * 64:h * 64 + 64, tile * 128:tile * 128 + 128] = jnp.where(low, first[h], then[h]).astype(bf16)

    def save(cur, qp, xp):
        for h in heads:
            xk_ref[h], xq_ref[h], xt_ref[h] = cur[0][h], cur[1][h], cur[2][h]
            xd_ref[0, h], xd_ref[1, h], xd_ref[2, h] = cur[3][h], cur[4][h], xp[h]
            rate_ref[h], xq_ref[nh + h] = cur[5][h], qp[h]

    def block(b, _):
        cur = ([xk_ref[h] for h in heads], [xq_ref[h] for h in heads], [xt_ref[h] for h in heads],
               [xd_ref[0, h] for h in heads], [xd_ref[1, h] for h in heads], [rate_ref[h] for h in heads])
        mid = prep(b, 1)
        ye, yo = tile_steps(cur, mid, [xq_ref[nh + h] for h in heads], [xd_ref[2, h] for h in heads])
        put(jnp.maximum(b - 1, 0), 1, [yprev_ref[h] for h in heads], ye)
        end = prep(jnp.minimum(b + 1, nb - 1), 0)
        ye, yn = tile_steps(mid, end, cur[1], cur[4])
        put(b, 0, yo, ye)
        for h in heads:
            yprev_ref[h] = yn[h]
        save(end, mid[1], mid[4])
        return 0

    first = prep(0, 0)
    zero = [jnp.zeros((64, 128), f32) for h in heads]
    none = [jnp.zeros((64, 256), bf16) for h in heads]
    for h in heads:
        xs = jnp.concatenate(tokmajor(first[0][h]), 1)
        base_ref[h] = dot(xs, stack4(*split(w1_ref[h]), 0)) + c1_ref[h]
    save(first, zero, none)
    lax.fori_loop(0, nb, block, 0)
    hid, _ = hidden([xd_ref[2, h] for h in heads])
    z = second(gelu(hid, None)[0], [split(w2_ref[h]) for h in heads])
    last = []
    for h in heads:
        c, rstd = normed(z[h])
        last.append(c * rstd * gain_ref[h] + xq_ref[nh + h] + shift_ref[h])
    put(nb - 1, 1, [yprev_ref[h] for h in heads], last)


def ttt(x, cos, sin, gain, shift, own):
    nh = gain.shape[0]
    return pl.pallas_call(
        ttt_kernel,
        out_shape=jax.ShapeDtypeStruct((x.shape[0], nh * 64, x.shape[2]), bf16),
        in_specs=[pl.BlockSpec(memory_space=pltpu.VMEM)] * 6,
        out_specs=pl.BlockSpec(memory_space=pltpu.VMEM),
        scratch_shapes=[
            pltpu.VMEM((nh, 64, 256), f32),
            pltpu.VMEM((nh, 1, 256), f32),
            pltpu.VMEM((nh, 64, 256), f32),
            pltpu.VMEM((nh, 64, 128), f32),
            pltpu.VMEM((nh, 64, 128), f32),
            pltpu.VMEM((nh, 128, 256), f32),
            pltpu.VMEM((nh, 128, 256), bf16),
            pltpu.VMEM((nh, 128, 256), bf16),
            pltpu.VMEM((nh, 64, 128), f32),
            pltpu.VMEM((2 * nh, 64, 128), f32),
            pltpu.VMEM((nh, 64, 128), f32),
            pltpu.VMEM((3, nh, 64, 256), bf16),
            pltpu.VMEM((nh, 1, 128), f32),
        ],
        compiler_params=pltpu.CompilerParams(vmem_limit_bytes=48 * 1024 * 1024),
    )(x, cos, sin, gain, shift, own)


def pack_kernel(w1_ref, c1_ref, w2_ref, c2_ref, out_ref):
    nh = w1_ref.shape[0]
    c1, c2 = c1_ref[...], c2_ref[...]
    for h in range(nh):
        hl = slice(h * 256, h * 256 + 256)
        w2 = jnp.transpose(w2_ref[h])
        for i in range(8):
            out_ref[i, :, hl] = w1_ref[h, i * 8:i * 8 + 8]
            out_ref[8 + i, :, hl] = w2[i * 8:i * 8 + 8]
    out_ref[:, :, nh * 256:] = jnp.zeros_like(out_ref[:, :, nh * 256:])
    for i in range(16):
        out_ref[i, :nh, nh * 256:] = c1[:, :128]
        out_ref[i, nh:2 * nh, nh * 256:] = c1[:, 128:]
        for h in range(nh):
            at = nh * 256 + h % 2 * 64
            out_ref[i, 2 * nh + h // 2:2 * nh + h // 2 + 1, at:at + 64] = c2[h:h + 1]


def pack(w1, c1, w2, c2):
    return pl.pallas_call(
        pack_kernel,
        out_shape=jax.ShapeDtypeStruct((16, 8, w1.shape[0] * 256 + 128), f32),
        in_specs=[pl.BlockSpec(memory_space=pltpu.VMEM)] * 4,
        out_specs=pl.BlockSpec(memory_space=pltpu.VMEM),
        compiler_params=pltpu.CompilerParams(vmem_limit_bytes=16 * 1024 * 1024),
    )(w1, c1, w2, c2)


def tables(off, n):
    half = 32
    freqs = jnp.exp(-jnp.log(10000.0) * jnp.arange(half, dtype=f32) / half)
    pos = (off + jnp.arange(n, dtype=jnp.int32)).astype(f32)
    ang = pos.reshape(n // 256, 1, 256) * freqs[None, :, None]
    return jnp.cos(ang), jnp.sin(ang)


def body(
    query_proj,
    key_proj,
    value_proj,
    learn_rate,
    norm_gain,
    norm_shift,
    start_offset,
    owner_map,
    first_weight,
    first_bias,
    second_weight,
    second_bias,
):
    groups = lax.axis_size("seq")
    nh, tok = first_weight.shape[1], query_proj.shape[1]

    packed = pack(first_weight[0], first_bias[0], second_weight[0], second_bias[0])
    held = lax.all_to_all(packed, "branch", split_axis=0, concat_axis=0, tiled=True)
    picked = held.at[owner_map].get(mode="promise_in_bounds")
    own = lax.all_to_all(picked, "branch", split_axis=0, concat_axis=0, tiled=True)

    def column(x):
        return jnp.broadcast_to(x[:, :, None], x.shape + (128,))

    def by_group(x):
        return x[0].T.reshape(groups, x.shape[2] // groups, tok)

    rates = jnp.pad(by_group(learn_rate), ((0, 0), (0, 16 - nh), (0, 0)))
    x = jnp.concatenate([by_group(query_proj), by_group(key_proj), by_group(value_proj), rates], 1)
    x = lax.all_to_all(x, "seq", split_axis=0, concat_axis=0, tiled=True)
    cos, sin = tables(start_offset[0], groups * tok)
    y = ttt(x, cos, sin, column(norm_gain), column(norm_shift), own)
    y = lax.all_to_all(y, "seq", split_axis=0, concat_axis=0, tiled=True)
    return y.reshape(groups * nh * 64, tok).T[None]


def solution(mesh):
    return jax.shard_map(
        body,
        mesh=mesh,
        in_specs=(
            P("branch", "seq", None),
            P("branch", "seq", None),
            P("branch", "seq", None),
            P("branch", "seq", None),
            P("seq", None),
            P("seq", None),
            P("branch"),
            P(),
            P("branch", "seq", None, None),
            P("branch", "seq", None),
            P("branch", "seq", None, None),
            P("branch", "seq", None),
        ),
        out_specs=P("branch", "seq", None),
        check_vma=False,
    )
```

```python
import jax
import jax.numpy as jnp
from jax import lax
from jax.experimental import pallas as pl
from jax.experimental.pallas import tpu as pltpu
from jax.sharding import PartitionSpec as P

f32, bf16 = jnp.float32, jnp.bfloat16
C0 = 0.7978845608028654
C1 = 0.044715
MB = 64
UNROLL = 2
SKEW = 2.0
ORDER = (("prep", 0), ("upd", 1), ("gelu", 2), ("w2", 3), ("z", 4), ("w1", 5), ("x", 6), ("base", 7), ("corr", 8),
         ("ln", 9), ("t", 10), ("da", 11), ("dh", 12), ("dw2", 13), ("state", 14), ("y", 15))


def split(x):
    hi = x.astype(bf16)
    return hi, (x - hi.astype(f32)).astype(bf16)


def stack4(hi, lo, axis):
    return jnp.concatenate([hi, lo, hi, lo], axis)


def dot(a, b):
    return jnp.dot(a, b, preferred_element_type=f32)


def dot_nt(a, b):
    return lax.dot_general(a, b, (((1,), (1,)), ((), ())), preferred_element_type=f32)


def ttt_kernel(x_ref, cos_ref, sin_ref, gain_ref, shift_ref, own_ref, out_ref,
               w1_ref, c1_ref, w2_ref, c2_ref, yprev_ref, base_ref, corr_ref, dh_ref,
               xk_ref, xq_ref, xt_ref, xd_ref, rate_ref):
    nh = w1_ref.shape[0]
    heads = range(nh)
    nb = x_ref.shape[0]
    rows = nh * 64
    for h in heads:
        hl = slice(h * 256, h * 256 + 256)
        for i in range(8):
            w1_ref[h, i * 8:i * 8 + 8] = own_ref[i, :, hl]
        w2 = jnp.concatenate([own_ref[8 + i, :, hl] for i in range(8)], 0)
        w2_ref[h] = 0.5 * (w2 - jnp.mean(w2, 0, keepdims=True))
        bias = own_ref[0, :, nh * 256:nh * 256 + 128]
        c1_ref[h] = jnp.concatenate([bias[h:h + 1], bias[nh + h:nh + h + 1]], 1)
        c2 = bias[2 * nh + h // 2:2 * nh + h // 2 + 1, h % 2 * 64:h % 2 * 64 + 64]
        c2_ref[h] = jnp.transpose(jnp.broadcast_to(c2 - jnp.mean(c2), (128, 64)))
    yprev_ref[...] = jnp.zeros_like(yprev_ref)
    dh_ref[...] = jnp.zeros_like(dh_ref)
    corr_ref[...] = jnp.zeros_like(corr_ref)
    low = lax.broadcasted_iota(jnp.int32, (64, 128), 1) < 64
    low1 = lax.broadcasted_iota(jnp.int32, (1, 128), 1) < 64

    def tokmajor(x):
        return split(jnp.transpose(jnp.concatenate([x, x], 0)))

    def rot(x, cs, sn):
        a, b = x[:32], x[32:]
        return jnp.concatenate([a * cs - b * sn, a * sn + b * cs], 0)

    def prep(b, tile, h):
        ts = slice(tile * 128, tile * 128 + 128)
        cs, sn = cos_ref[b, :, ts], sin_ref[b, :, ts]
        rates = x_ref[b, 3 * rows:3 * rows + 16, ts].astype(f32) * (1.0 / MB)
        q = rot(x_ref[b, h * 64:h * 64 + 64, ts].astype(f32), cs, sn)
        k = rot(x_ref[b, rows + h * 64:rows + h * 64 + 64, ts].astype(f32), cs, sn)
        v = x_ref[b, 2 * rows + h * 64:2 * rows + h * 64 + 64, ts].astype(f32)
        target = gain_ref[h] * (shift_ref[h] - (v - k))
        target = target - jnp.mean(target, 0, keepdims=True)
        kr = pltpu.roll(k, 64, 1)
        even = split(jnp.where(low, k, kr))
        odd = split(jnp.where(low, kr, k))
        return k, q, target, jnp.concatenate(even, 1), jnp.concatenate(odd, 1), rates[h:h + 1]

    refs = dict(w1=w1_ref, c1=c1_ref, w2=w2_ref, c2=c2_ref, base=base_ref, corr=corr_ref, dh=dh_ref)
    live = {}

    def load():
        for name, ref in refs.items():
            live[name] = [ref[h] for h in heads]

    def store():
        for name, ref in refs.items():
            for h in heads:
                ref[h] = live[name][h]

    def normed(z):
        c = z - jnp.mean(z, 0, keepdims=True)
        return c, lax.rsqrt(jnp.mean(c * c, 0, keepdims=True) + 1e-06)

    def hidden(h, xd):
        dh = live["dh"][h]
        upd = dot(jnp.concatenate([live["corr"][h], xd], 0), stack4(dh[:64], dh[64:], 0))
        return live["base"][h] - upd[:128], upd[128:]

    def gelu(x, sl):
        sq = x * x
        th = jnp.tanh(x * (sq * (C0 * C1) + C0))
        act = split(x * th + x)
        if sl is None:
            return act, None
        t, v = th[sl], x[sl]
        return act, (1.0 + t) * ((v * (sq[sl] * (3 * C0 * C1) + C0)) * (1.0 - t) + 1.0)

    def second(h, act, w2):
        z = dot_nt(jnp.concatenate(w2, 0), jnp.concatenate(act, 0))
        return (z[:64, :128] + z[64:, 128:]) + (z[64:, :128] + z[:64, 128:]) + live["c2"][h]

    def step(b, tile, even, cur, last, nxt):
        sl = slice(0, 64) if even else slice(64, 128)
        vs = [{} for h in heads]

        def s_upd(h, v):
            k, q, target, xe, xo, rate = cur[h]
            v["hid"], v["dw1"] = hidden(h, last[h][4] if even else xe)

        def s_gelu(h, v):
            v["act"], v["slope"] = gelu(v["hid"], sl)

        def s_w2(h, v):
            v["w2"] = split(live["w2"][h])

        def s_z(h, v):
            v["z"] = second(h, v["act"], v["w2"])

        def s_w1(h, v):
            v["w1"] = live["w1"][h] - v["dw1"]
            v["c1"] = live["c1"][h]

        def s_x(h, v):
            x = jnp.where(low, cur[h][1], cur[h][0]) if even else jnp.where(low, nxt[h][0], cur[h][1])
            v["x"] = jnp.concatenate(tokmajor(x), 1)

        def s_base(h, v):
            live["base"][h] = dot(v["x"], stack4(*split(v["w1"]), 0)) + v["c1"]

        def s_corr(h, v):
            xd = cur[h][3 if even else 4]
            live["corr"][h] = jnp.concatenate(split(dot(v["x"], stack4(xd[:, :128], xd[:, 128:], 0)) + 1.0), 1)

        def s_ln(h, v):
            c, rstd = normed(v["z"])
            gain, target = gain_ref[h], cur[h][2]
            rate = jnp.where(low1, cur[h][5], 0.0) if even else jnp.where(low1, 0.0, cur[h][5])
            v["c"], v["rstd"] = c, rstd
            g2c = gain * gain * c
            m2 = jnp.mean(g2c, 0, keepdims=True)
            m3 = jnp.mean(g2c * c, 0, keepdims=True)
            m4 = jnp.mean(target * c, 0, keepdims=True)
            e = rstd * rstd * (rstd * m3 + m4)
            v["dz"] = rstd * rate * ((g2c - m2) * rstd + target - c * e)

        def s_t(h, v):
            hi, lo = tokmajor(v["dz"])
            v["dzt"] = jnp.concatenate([hi[sl], lo[sl]], 1)

        def s_da(h, v):
            v["da"] = dot(v["dzt"], stack4(*v["w2"], 0))

        def s_dh(h, v):
            v["dh"] = v["da"] * v["slope"]
            live["dh"][h] = jnp.concatenate(split(v["dh"]), 0)

        def s_dw2(h, v):
            d = v["dz"] + pltpu.roll(v["dz"], 64, 1)
            dw2 = dot(jnp.concatenate(split(d), 1), stack4(v["act"][0][sl], v["act"][1][sl], 0))
            live["w2"][h] = live["w2"][h] - 0.25 * dw2
            live["c2"][h] = live["c2"][h] - jnp.sum(v["dz"], 1, keepdims=True)

        def s_state(h, v):
            live["w1"][h] = v["w1"]
            live["c1"][h] = v["c1"] - jnp.sum(v["dh"], 0, keepdims=True)

        def s_y(h, v):
            q = last[h][1] if even else cur[h][1]
            v["y"] = v["c"] * v["rstd"] * gain_ref[h] + (q + shift_ref[h])

        def s_prep(h, v):
            if even:
                nxt[h] = prep(b, tile, h)

        stages = dict(upd=s_upd, gelu=s_gelu, w2=s_w2, z=s_z, w1=s_w1, x=s_x, base=s_base, corr=s_corr, ln=s_ln,
                      t=s_t, da=s_da, dh=s_dh, dw2=s_dw2, state=s_state, y=s_y, prep=s_prep)
        order = sorted((at + SKEW * h, i, h, name) for i, (name, at) in enumerate(ORDER) for h in heads)
        for _, _, h, name in order:
            stages[name](h, vs[h])
        return [v["y"] for v in vs]

    def put(b, tile, first, then):
        for h in heads:
            out_ref[b, h * 64:h * 64 + 64, tile * 128:tile * 128 + 128] = jnp.where(low, first[h], then[h]).astype(bf16)

    def save(cur, last):
        for h in heads:
            xk_ref[h], xq_ref[h], xt_ref[h] = cur[h][0], cur[h][1], cur[h][2]
            xd_ref[0, h], xd_ref[1, h], xd_ref[2, h] = cur[h][3], cur[h][4], last[h][4]
            rate_ref[h], xq_ref[nh + h] = cur[h][5], last[h][1]

    def block(b, _):
        load()
        cur = [(xk_ref[h], xq_ref[h], xt_ref[h], xd_ref[0, h], xd_ref[1, h], rate_ref[h]) for h in heads]
        last = [(None, xq_ref[nh + h], None, None, xd_ref[2, h], None) for h in heads]
        mid, end = [None] * nh, [None] * nh
        y = step(b, 1, True, cur, last, mid)
        put(jnp.maximum(b - 1, 0), 1, [yprev_ref[h] for h in heads], y)
        first = step(b, 1, False, cur, last, mid)
        then = step(jnp.minimum(b + 1, nb - 1), 0, True, mid, cur, end)
        put(b, 0, first, then)
        y = step(b, 0, False, mid, cur, end)
        for h in heads:
            yprev_ref[h] = y[h]
        save(end, mid)
        store()
        return 0

    first = [prep(0, 0, h) for h in heads]
    for h in heads:
        xs = jnp.concatenate(tokmajor(first[h][0]), 1)
        base_ref[h] = dot(xs, stack4(*split(w1_ref[h]), 0)) + c1_ref[h]
    save(first, [(None, jnp.zeros((64, 128), f32), None, None, jnp.zeros((64, 256), bf16), None)] * nh)
    lax.fori_loop(0, nb, block, 0, unroll=UNROLL)
    load()
    y = []
    for h in heads:
        hid, _ = hidden(h, xd_ref[2, h])
        c, rstd = normed(second(h, gelu(hid, None)[0], split(live["w2"][h])))
        y.append(c * rstd * gain_ref[h] + (xq_ref[nh + h] + shift_ref[h]))
    put(nb - 1, 1, [yprev_ref[h] for h in heads], y)


def ttt(x, cos, sin, gain, shift, own):
    nh = gain.shape[0]
    return pl.pallas_call(
        ttt_kernel,
        out_shape=jax.ShapeDtypeStruct((x.shape[0], nh * 64, x.shape[2]), bf16),
        in_specs=[pl.BlockSpec(memory_space=pltpu.VMEM)] * 6,
        out_specs=pl.BlockSpec(memory_space=pltpu.VMEM),
        scratch_shapes=[
            pltpu.VMEM((nh, 64, 256), f32),
            pltpu.VMEM((nh, 1, 256), f32),
            pltpu.VMEM((nh, 64, 256), f32),
            pltpu.VMEM((nh, 64, 128), f32),
            pltpu.VMEM((nh, 64, 128), f32),
            pltpu.VMEM((nh, 128, 256), f32),
            pltpu.VMEM((nh, 128, 256), bf16),
            pltpu.VMEM((nh, 128, 256), bf16),
            pltpu.VMEM((nh, 64, 128), f32),
            pltpu.VMEM((2 * nh, 64, 128), f32),
            pltpu.VMEM((nh, 64, 128), f32),
            pltpu.VMEM((3, nh, 64, 256), bf16),
            pltpu.VMEM((nh, 1, 128), f32),
        ],
        compiler_params=pltpu.CompilerParams(vmem_limit_bytes=48 * 1024 * 1024),
    )(x, cos, sin, gain, shift, own)


def pack_kernel(w1_ref, c1_ref, w2_ref, c2_ref, out_ref):
    nh = w1_ref.shape[0]
    c1, c2 = c1_ref[...], c2_ref[...]
    for h in range(nh):
        hl = slice(h * 256, h * 256 + 256)
        w2 = jnp.transpose(w2_ref[h])
        for i in range(8):
            out_ref[i, :, hl] = w1_ref[h, i * 8:i * 8 + 8]
            out_ref[8 + i, :, hl] = w2[i * 8:i * 8 + 8]
    out_ref[:, :, nh * 256:] = jnp.zeros_like(out_ref[:, :, nh * 256:])
    for i in range(16):
        out_ref[i, :nh, nh * 256:] = c1[:, :128]
        out_ref[i, nh:2 * nh, nh * 256:] = c1[:, 128:]
        for h in range(nh):
            at = nh * 256 + h % 2 * 64
            out_ref[i, 2 * nh + h // 2:2 * nh + h // 2 + 1, at:at + 64] = c2[h:h + 1]


def pack(w1, c1, w2, c2):
    return pl.pallas_call(
        pack_kernel,
        out_shape=jax.ShapeDtypeStruct((16, 8, w1.shape[0] * 256 + 128), f32),
        in_specs=[pl.BlockSpec(memory_space=pltpu.VMEM)] * 4,
        out_specs=pl.BlockSpec(memory_space=pltpu.VMEM),
        compiler_params=pltpu.CompilerParams(vmem_limit_bytes=16 * 1024 * 1024),
    )(w1, c1, w2, c2)


def tables(off, n):
    half = 32
    freqs = jnp.exp(-jnp.log(10000.0) * jnp.arange(half, dtype=f32) / half)
    pos = (off + jnp.arange(n, dtype=jnp.int32)).astype(f32)
    ang = pos.reshape(n // 256, 1, 256) * freqs[None, :, None]
    return jnp.cos(ang), jnp.sin(ang)


def body(
    query_proj,
    key_proj,
    value_proj,
    learn_rate,
    norm_gain,
    norm_shift,
    start_offset,
    owner_map,
    first_weight,
    first_bias,
    second_weight,
    second_bias,
):
    groups = lax.axis_size("seq")
    nh, tok = first_weight.shape[1], query_proj.shape[1]

    packed = pack(first_weight[0], first_bias[0], second_weight[0], second_bias[0])
    held = lax.all_to_all(packed, "branch", split_axis=0, concat_axis=0, tiled=True)
    picked = held.at[owner_map].get(mode="promise_in_bounds")
    own = lax.all_to_all(picked, "branch", split_axis=0, concat_axis=0, tiled=True)

    def column(x):
        return jnp.broadcast_to(x[:, :, None], x.shape + (128,))

    def by_group(x):
        return x[0].T.reshape(groups, x.shape[2] // groups, tok)

    rates = jnp.pad(by_group(learn_rate), ((0, 0), (0, 16 - nh), (0, 0)))
    x = jnp.concatenate([by_group(query_proj), by_group(key_proj), by_group(value_proj), rates], 1)
    x = lax.all_to_all(x, "seq", split_axis=0, concat_axis=0, tiled=True)
    cos, sin = tables(start_offset[0], groups * tok)
    y = ttt(x, cos, sin, column(norm_gain), column(norm_shift), own)
    y = lax.all_to_all(y, "seq", split_axis=0, concat_axis=0, tiled=True)
    return y.reshape(groups * nh * 64, tok).T[None]


def solution(mesh):
    return jax.shard_map(
        body,
        mesh=mesh,
        in_specs=(
            P("branch", "seq", None),
            P("branch", "seq", None),
            P("branch", "seq", None),
            P("branch", "seq", None),
            P("seq", None),
            P("seq", None),
            P("branch"),
            P(),
            P("branch", "seq", None, None),
            P("branch", "seq", None),
            P("branch", "seq", None, None),
            P("branch", "seq", None),
        ),
        out_specs=P("branch", "seq", None),
        check_vma=False,
    )
```

```python
import jax
import jax.numpy as jnp
from jax import lax
from jax.experimental import pallas as pl
from jax.experimental.pallas import tpu as pltpu
from jax.sharding import PartitionSpec as P

f32, bf16 = jnp.float32, jnp.bfloat16
C0 = 0.7978845608028654
C1 = 0.044715
MB = 64
UNROLL = 2
SKEW = 2.0
ORDER = (("prep", 0), ("upd", 1), ("gelu", 2), ("w2", 3), ("z", 4), ("w1", 5), ("x", 6), ("base", 7), ("corr", 8),
         ("ln", 9), ("t", 10), ("da", 11), ("dh", 12), ("dw2", 13), ("state", 14), ("y", 15))


def split(x):
    hi = x.astype(bf16)
    return hi, (x - hi.astype(f32)).astype(bf16)


def stack4(hi, lo, axis):
    return jnp.concatenate([hi, lo, hi, lo], axis)


def dot(a, b):
    return jnp.dot(a, b, preferred_element_type=f32)


def dot_nt(a, b):
    return lax.dot_general(a, b, (((1,), (1,)), ((), ())), preferred_element_type=f32)


def ttt_kernel(x_ref, cos_ref, sin_ref, gain_ref, shift_ref, own_ref, out_ref,
               w1_ref, c1_ref, w2_ref, c2_ref, yprev_ref, base_ref, corr_ref, dh_ref,
               xk_ref, xq_ref, xt_ref, xd_ref, rate_ref):
    nh = w1_ref.shape[0]
    heads = range(nh)
    nb = x_ref.shape[0]
    rows = nh * 64
    for h in heads:
        hl = slice(h * 256, h * 256 + 256)
        for i in range(8):
            w1_ref[h, i * 8:i * 8 + 8] = own_ref[i, :, hl]
        w2 = jnp.concatenate([own_ref[8 + i, :, hl] for i in range(8)], 0)
        w2_ref[h] = 0.5 * (w2 - jnp.mean(w2, 0, keepdims=True))
        bias = own_ref[0, :, nh * 256:nh * 256 + 128]
        c1_ref[h] = jnp.concatenate([bias[h:h + 1], bias[nh + h:nh + h + 1]], 1)
        c2 = bias[2 * nh + h // 2:2 * nh + h // 2 + 1, h % 2 * 64:h % 2 * 64 + 64]
        c2_ref[h] = jnp.transpose(jnp.broadcast_to(c2 - jnp.mean(c2), (128, 64)))
    yprev_ref[...] = jnp.zeros_like(yprev_ref)
    dh_ref[...] = jnp.zeros_like(dh_ref)
    corr_ref[...] = jnp.zeros_like(corr_ref)
    low = lax.broadcasted_iota(jnp.int32, (64, 128), 1) < 64
    low1 = lax.broadcasted_iota(jnp.int32, (1, 128), 1) < 64

    def tokmajor(x):
        return split(jnp.transpose(jnp.concatenate([x, x], 0)))

    def rot(x, cs, sn):
        a, b = x[:32], x[32:]
        return jnp.concatenate([a * cs - b * sn, a * sn + b * cs], 0)

    def prep(b, tile, h):
        ts = slice(tile * 128, tile * 128 + 128)
        cs, sn = cos_ref[b, :, ts], sin_ref[b, :, ts]
        rates = x_ref[b, 3 * rows:3 * rows + 16, ts].astype(f32) * (1.0 / MB)
        q = rot(x_ref[b, h * 64:h * 64 + 64, ts].astype(f32), cs, sn)
        k = rot(x_ref[b, rows + h * 64:rows + h * 64 + 64, ts].astype(f32), cs, sn)
        v = x_ref[b, 2 * rows + h * 64:2 * rows + h * 64 + 64, ts].astype(f32)
        target = gain_ref[h] * (shift_ref[h] - (v - k))
        target = target - jnp.mean(target, 0, keepdims=True)
        kr = pltpu.roll(k, 64, 1)
        even = split(jnp.where(low, k, kr))
        odd = split(jnp.where(low, kr, k))
        return k, q, target, jnp.concatenate(even, 1), jnp.concatenate(odd, 1), rates[h:h + 1]

    refs = dict(w1=w1_ref, c1=c1_ref, w2=w2_ref, c2=c2_ref, base=base_ref, corr=corr_ref, dh=dh_ref)
    live = {}

    def load():
        for name, ref in refs.items():
            live[name] = [ref[h] for h in heads]

    def store():
        for name, ref in refs.items():
            for h in heads:
                ref[h] = live[name][h]

    def normed(z):
        c = z - jnp.mean(z, 0, keepdims=True)
        return c, lax.rsqrt(jnp.mean(c * c, 0, keepdims=True) + 1e-06)

    def hidden(h, xd):
        dh = live["dh"][h]
        upd = dot(jnp.concatenate([live["corr"][h], xd], 0), stack4(dh[:64], dh[64:], 0))
        return live["base"][h] - upd[:128], upd[128:]

    def gelu(x, sl):
        sq = x * x
        th = jnp.tanh(x * (sq * (C0 * C1) + C0))
        act = split(x * th + x)
        if sl is None:
            return act, None
        t, v = th[sl], x[sl]
        return act, (1.0 + t) * ((v * (sq[sl] * (3 * C0 * C1) + C0)) * (1.0 - t) + 1.0)

    def second(h, act, w2):
        z = dot_nt(jnp.concatenate(w2, 0), jnp.concatenate(act, 0))
        return (z[:64, :128] + z[64:, 128:]) + (z[64:, :128] + z[:64, 128:]) + live["c2"][h]

    def step(b, tile, even, cur, last, nxt):
        sl = slice(0, 64) if even else slice(64, 128)
        vs = [{} for h in heads]

        def s_upd(h, v):
            k, q, target, xe, xo, rate = cur[h]
            v["hid"], v["dw1"] = hidden(h, last[h][4] if even else xe)

        def s_gelu(h, v):
            v["act"], v["slope"] = gelu(v["hid"], sl)

        def s_w2(h, v):
            v["w2"] = split(live["w2"][h])

        def s_z(h, v):
            v["z"] = second(h, v["act"], v["w2"])

        def s_w1(h, v):
            v["w1"] = live["w1"][h] - v["dw1"]
            v["c1"] = live["c1"][h]

        def s_x(h, v):
            x = jnp.where(low, cur[h][1], cur[h][0]) if even else jnp.where(low, nxt[h][0], cur[h][1])
            v["x"] = jnp.concatenate(tokmajor(x), 1)

        def s_base(h, v):
            live["base"][h] = dot(v["x"], stack4(*split(v["w1"]), 0)) + v["c1"]

        def s_corr(h, v):
            xd = cur[h][3 if even else 4]
            live["corr"][h] = jnp.concatenate(split(dot(v["x"], stack4(xd[:, :128], xd[:, 128:], 0)) + 1.0), 1)

        def s_ln(h, v):
            c, rstd = normed(v["z"])
            gain, target = gain_ref[h], cur[h][2]
            rate = jnp.where(low1, cur[h][5], 0.0) if even else jnp.where(low1, 0.0, cur[h][5])
            v["c"], v["rstd"] = c, rstd
            g2c = gain * gain * c
            m2 = jnp.mean(g2c, 0, keepdims=True)
            m3 = jnp.mean(g2c * c, 0, keepdims=True)
            m4 = jnp.mean(target * c, 0, keepdims=True)
            e = rstd * rstd * (rstd * m3 + m4)
            v["dz"] = rstd * rate * ((g2c - m2) * rstd + target - c * e)

        def s_t(h, v):
            v["dzt"] = jnp.concatenate([jnp.transpose(jnp.concatenate([x, x], 0))[sl] for x in split(v["dz"])], 1)

        def s_da(h, v):
            v["da"] = dot(v["dzt"], stack4(*v["w2"], 0))

        def s_dh(h, v):
            v["dh"] = v["da"] * v["slope"]
            live["dh"][h] = jnp.concatenate(split(v["dh"]), 0)

        def s_dw2(h, v):
            d = v["dz"] + pltpu.roll(v["dz"], 64, 1)
            dw2 = dot(jnp.concatenate(split(d), 1), stack4(v["act"][0][sl], v["act"][1][sl], 0))
            live["w2"][h] = live["w2"][h] - 0.25 * dw2
            live["c2"][h] = live["c2"][h] - jnp.sum(v["dz"], 1, keepdims=True)

        def s_state(h, v):
            live["w1"][h] = v["w1"]
            live["c1"][h] = v["c1"] - jnp.sum(v["dh"], 0, keepdims=True)

        def s_y(h, v):
            q = last[h][1] if even else cur[h][1]
            v["y"] = v["c"] * v["rstd"] * gain_ref[h] + (q + shift_ref[h])

        def s_prep(h, v):
            if even:
                nxt[h] = prep(b, tile, h)

        stages = dict(upd=s_upd, gelu=s_gelu, w2=s_w2, z=s_z, w1=s_w1, x=s_x, base=s_base, corr=s_corr, ln=s_ln,
                      t=s_t, da=s_da, dh=s_dh, dw2=s_dw2, state=s_state, y=s_y, prep=s_prep)
        order = sorted((at + SKEW * h, i, h, name) for i, (name, at) in enumerate(ORDER) for h in heads)
        for _, _, h, name in order:
            stages[name](h, vs[h])
        return [v["y"] for v in vs]

    def put(b, tile, first, then):
        for h in heads:
            out_ref[b, h * 64:h * 64 + 64, tile * 128:tile * 128 + 128] = jnp.where(low, first[h], then[h]).astype(bf16)

    def save(cur, last):
        for h in heads:
            xk_ref[h], xq_ref[h], xt_ref[h] = cur[h][0], cur[h][1], cur[h][2]
            xd_ref[0, h], xd_ref[1, h], xd_ref[2, h] = cur[h][3], cur[h][4], last[h][4]
            rate_ref[h], xq_ref[nh + h] = cur[h][5], last[h][1]

    def block(b, _):
        load()
        cur = [(xk_ref[h], xq_ref[h], xt_ref[h], xd_ref[0, h], xd_ref[1, h], rate_ref[h]) for h in heads]
        last = [(None, xq_ref[nh + h], None, None, xd_ref[2, h], None) for h in heads]
        mid, end = [None] * nh, [None] * nh
        y = step(b, 1, True, cur, last, mid)
        put(jnp.maximum(b - 1, 0), 1, [yprev_ref[h] for h in heads], y)
        first = step(b, 1, False, cur, last, mid)
        then = step(jnp.minimum(b + 1, nb - 1), 0, True, mid, cur, end)
        put(b, 0, first, then)
        y = step(b, 0, False, mid, cur, end)
        for h in heads:
            yprev_ref[h] = y[h]
        save(end, mid)
        store()
        return 0

    first = [prep(0, 0, h) for h in heads]
    for h in heads:
        xs = jnp.concatenate(tokmajor(first[h][0]), 1)
        base_ref[h] = dot(xs, stack4(*split(w1_ref[h]), 0)) + c1_ref[h]
    save(first, [(None, jnp.zeros((64, 128), f32), None, None, jnp.zeros((64, 256), bf16), None)] * nh)
    lax.fori_loop(0, nb, block, 0, unroll=UNROLL)
    load()
    y = []
    for h in heads:
        hid, _ = hidden(h, xd_ref[2, h])
        c, rstd = normed(second(h, gelu(hid, None)[0], split(live["w2"][h])))
        y.append(c * rstd * gain_ref[h] + (xq_ref[nh + h] + shift_ref[h]))
    put(nb - 1, 1, [yprev_ref[h] for h in heads], y)


def ttt(x, cos, sin, gain, shift, own):
    nh = gain.shape[0]
    return pl.pallas_call(
        ttt_kernel,
        out_shape=jax.ShapeDtypeStruct((x.shape[0], nh * 64, x.shape[2]), bf16),
        in_specs=[pl.BlockSpec(memory_space=pltpu.VMEM)] * 6,
        out_specs=pl.BlockSpec(memory_space=pltpu.VMEM),
        scratch_shapes=[
            pltpu.VMEM((nh, 64, 256), f32),
            pltpu.VMEM((nh, 1, 256), f32),
            pltpu.VMEM((nh, 64, 256), f32),
            pltpu.VMEM((nh, 64, 128), f32),
            pltpu.VMEM((nh, 64, 128), f32),
            pltpu.VMEM((nh, 128, 256), f32),
            pltpu.VMEM((nh, 128, 256), bf16),
            pltpu.VMEM((nh, 128, 256), bf16),
            pltpu.VMEM((nh, 64, 128), f32),
            pltpu.VMEM((2 * nh, 64, 128), f32),
            pltpu.VMEM((nh, 64, 128), f32),
            pltpu.VMEM((3, nh, 64, 256), bf16),
            pltpu.VMEM((nh, 1, 128), f32),
        ],
        compiler_params=pltpu.CompilerParams(vmem_limit_bytes=48 * 1024 * 1024),
    )(x, cos, sin, gain, shift, own)


def pack_kernel(w1_ref, c1_ref, w2_ref, c2_ref, out_ref):
    nh = w1_ref.shape[1]
    c1 = jnp.concatenate([c1_ref[h] for h in range(nh)], 0)
    for h in range(nh):
        hl = slice(h * 256, h * 256 + 256)
        for i in range(8):
            out_ref[i, :, hl] = w1_ref[0, h, i * 8:i * 8 + 8]
            out_ref[8 + i, :, hl] = w2_ref[0, h, i * 8:i * 8 + 8]
    out_ref[:, :, nh * 256:] = jnp.zeros_like(out_ref[:, :, nh * 256:])
    for i in range(16):
        out_ref[i, :nh, nh * 256:] = c1[:, :128]
        out_ref[i, nh:2 * nh, nh * 256:] = c1[:, 128:]
        for h in range(nh):
            at = nh * 256 + h % 2 * 64
            out_ref[i, 2 * nh + h // 2:2 * nh + h // 2 + 1, at:at + 64] = c2_ref[h]


def pack(w1, c1, w2, c2):
    return pl.pallas_call(
        pack_kernel,
        out_shape=jax.ShapeDtypeStruct((16, 8, w1.shape[1] * 256 + 128), f32),
        in_specs=[pl.BlockSpec(memory_space=pltpu.VMEM)] * 4,
        out_specs=pl.BlockSpec(memory_space=pltpu.VMEM),
        compiler_params=pltpu.CompilerParams(vmem_limit_bytes=16 * 1024 * 1024),
    )(w1, c1, w2, c2)


def tables(off, n):
    half = 32
    freqs = jnp.exp(-jnp.log(10000.0) * jnp.arange(half, dtype=f32) / half)
    pos = (off + jnp.arange(n, dtype=jnp.int32)).astype(f32)
    ang = pos.reshape(n // 256, 1, 256) * freqs[None, :, None]
    return jnp.cos(ang), jnp.sin(ang)


def body(
    query_proj,
    key_proj,
    value_proj,
    learn_rate,
    norm_gain,
    norm_shift,
    start_offset,
    owner_map,
    first_weight,
    first_bias,
    second_weight,
    second_bias,
):
    groups = lax.axis_size("seq")
    nh, tok = first_weight.shape[1], query_proj.shape[1]

    packed = pack(first_weight, jnp.swapaxes(first_bias, 0, 1), jnp.swapaxes(second_weight, 2, 3), jnp.swapaxes(second_bias, 0, 1))
    held = lax.all_to_all(packed, "branch", split_axis=0, concat_axis=0, tiled=True)
    picked = held.at[owner_map].get(mode="promise_in_bounds")
    own = lax.all_to_all(picked, "branch", split_axis=0, concat_axis=0, tiled=True)

    def column(x):
        return jnp.broadcast_to(x[:, :, None], x.shape + (128,))

    def by_group(x):
        return x[0].T.reshape(groups, x.shape[2] // groups, tok)

    rates = jnp.pad(by_group(learn_rate), ((0, 0), (0, 16 - nh), (0, 0)))
    x = jnp.concatenate([by_group(query_proj), by_group(key_proj), by_group(value_proj), rates], 1)
    x = lax.all_to_all(x, "seq", split_axis=0, concat_axis=0, tiled=True)
    cos, sin = tables(start_offset[0], groups * tok)
    y = ttt(x, cos, sin, column(norm_gain), column(norm_shift), own)
    y = lax.all_to_all(y, "seq", split_axis=0, concat_axis=0, tiled=True)
    return y.reshape(groups * nh * 64, tok).T[None]


def solution(mesh):
    return jax.shard_map(
        body,
        mesh=mesh,
        in_specs=(
            P("branch", "seq", None),
            P("branch", "seq", None),
            P("branch", "seq", None),
            P("branch", "seq", None),
            P("seq", None),
            P("seq", None),
            P("branch"),
            P(),
            P("branch", "seq", None, None),
            P("branch", "seq", None),
            P("branch", "seq", None, None),
            P("branch", "seq", None),
        ),
        out_specs=P("branch", "seq", None),
        check_vma=False,
    )
```

```python
import jax
import jax.numpy as jnp
from jax import lax
from jax.experimental import pallas as pl
from jax.experimental.pallas import tpu as pltpu
from jax.sharding import PartitionSpec as P

f32, bf16 = jnp.float32, jnp.bfloat16
C0 = 0.7978845608028654
C1 = 0.044715
MB = 64
UNROLL = 2
SKEW = 2.0
ORDER = (("prep", 0), ("upd", 1), ("gelu", 2), ("w2", 3), ("z", 4), ("w1", 5), ("x", 6), ("base", 7), ("corr", 8),
         ("ln", 9), ("t", 10), ("da", 11), ("dh", 12), ("dw2", 13), ("state", 14), ("y", 15))


def split(x):
    hi = x.astype(bf16)
    return hi, (x - hi.astype(f32)).astype(bf16)


def stack4(hi, lo, axis):
    return jnp.concatenate([hi, lo, hi, lo], axis)


def dot(a, b):
    return jnp.dot(a, b, preferred_element_type=f32)


def dot_nt(a, b):
    return lax.dot_general(a, b, (((1,), (1,)), ((), ())), preferred_element_type=f32)


def ttt_kernel(x_ref, cos_ref, sin_ref, gain_ref, shift_ref, own_ref, out_ref,
               w1_ref, c1_ref, w2_ref, c2_ref, yprev_ref, base_ref, corr_ref, dh_ref,
               xk_ref, xq_ref, xt_ref, xd_ref, rate_ref):
    nh = w1_ref.shape[0]
    heads = range(nh)
    nb = x_ref.shape[0]
    rows = nh * 64
    for h in heads:
        hl = slice(h * 256, h * 256 + 256)
        for i in range(8):
            w1_ref[h, i * 8:i * 8 + 8] = own_ref[i, :, hl]
        w2 = jnp.concatenate([own_ref[8 + i, :, hl] for i in range(8)], 0)
        w2_ref[h] = 0.5 * (w2 - jnp.mean(w2, 0, keepdims=True))
        bias = own_ref[0, :, nh * 256:nh * 256 + 128]
        c1_ref[h] = jnp.concatenate([bias[h:h + 1], bias[nh + h:nh + h + 1]], 1)
        c2 = bias[2 * nh + h // 2:2 * nh + h // 2 + 1, h % 2 * 64:h % 2 * 64 + 64]
        c2_ref[h] = jnp.transpose(jnp.broadcast_to(c2 - jnp.mean(c2), (128, 64)))
    yprev_ref[...] = jnp.zeros_like(yprev_ref)
    dh_ref[...] = jnp.zeros_like(dh_ref)
    corr_ref[...] = jnp.zeros_like(corr_ref)
    low = lax.broadcasted_iota(jnp.int32, (64, 128), 1) < 64
    low1 = lax.broadcasted_iota(jnp.int32, (1, 128), 1) < 64

    def tokmajor(x):
        return split(jnp.transpose(jnp.concatenate([x, x], 0)))

    def rot(x, cs, sn):
        a, b = x[:32], x[32:]
        return jnp.concatenate([a * cs - b * sn, a * sn + b * cs], 0)

    def prep(b, tile, h):
        ts = slice(tile * 128, tile * 128 + 128)
        cs, sn = cos_ref[b, :, ts], sin_ref[b, :, ts]
        rates = x_ref[b, 3 * rows:3 * rows + 16, ts].astype(f32) * (1.0 / MB)
        q = rot(x_ref[b, h * 64:h * 64 + 64, ts].astype(f32), cs, sn)
        k = rot(x_ref[b, rows + h * 64:rows + h * 64 + 64, ts].astype(f32), cs, sn)
        v = x_ref[b, 2 * rows + h * 64:2 * rows + h * 64 + 64, ts].astype(f32)
        target = gain_ref[h] * (shift_ref[h] - (v - k))
        target = target - jnp.mean(target, 0, keepdims=True)
        kr = pltpu.roll(k, 64, 1)
        even = split(jnp.where(low, k, kr))
        odd = split(jnp.where(low, kr, k))
        return k, q, target, jnp.concatenate(even, 1), jnp.concatenate(odd, 1), rates[h:h + 1]

    refs = dict(w1=w1_ref, c1=c1_ref, w2=w2_ref, c2=c2_ref, base=base_ref, corr=corr_ref, dh=dh_ref)
    live = {}

    def load():
        for name, ref in refs.items():
            live[name] = [ref[h] for h in heads]

    def store():
        for name, ref in refs.items():
            for h in heads:
                ref[h] = live[name][h]

    def normed(z):
        c = z - jnp.mean(z, 0, keepdims=True)
        return c, lax.rsqrt(jnp.mean(c * c, 0, keepdims=True) + 1e-06)

    def hidden(h, xd):
        dh = live["dh"][h]
        upd = dot(jnp.concatenate([live["corr"][h], xd], 0), stack4(dh[:64], dh[64:], 0))
        return live["base"][h] - upd[:128], upd[128:]

    def gelu(x, sl):
        sq = x * x
        th = jnp.tanh(x * (sq * (C0 * C1) + C0))
        act = split(x * th + x)
        if sl is None:
            return act, None
        t, v = th[sl], x[sl]
        return act, (1.0 + t) * ((v * (sq[sl] * (3 * C0 * C1) + C0)) * (1.0 - t) + 1.0)

    def second(h, act, w2):
        z = dot_nt(jnp.concatenate(w2, 0), jnp.concatenate(act, 0))
        return (z[:64, :128] + z[64:, 128:]) + (z[64:, :128] + z[:64, 128:]) + live["c2"][h]

    def step(b, tile, even, cur, last, nxt):
        sl = slice(0, 64) if even else slice(64, 128)
        vs = [{} for h in heads]

        def s_upd(h, v):
            k, q, target, xe, xo, rate = cur[h]
            v["hid"], v["dw1"] = hidden(h, last[h][4] if even else xe)

        def s_gelu(h, v):
            v["act"], v["slope"] = gelu(v["hid"], sl)

        def s_w2(h, v):
            v["w2"] = split(live["w2"][h])

        def s_z(h, v):
            v["z"] = second(h, v["act"], v["w2"])

        def s_w1(h, v):
            v["w1"] = live["w1"][h] - v["dw1"]
            v["c1"] = live["c1"][h]

        def s_x(h, v):
            x = jnp.where(low, cur[h][1], cur[h][0]) if even else jnp.where(low, nxt[h][0], cur[h][1])
            v["x"] = jnp.concatenate(tokmajor(x), 1)

        def s_base(h, v):
            live["base"][h] = dot(v["x"], stack4(*split(v["w1"]), 0)) + v["c1"]

        def s_corr(h, v):
            xd = cur[h][3 if even else 4]
            live["corr"][h] = jnp.concatenate(split(dot(v["x"], stack4(xd[:, :128], xd[:, 128:], 0)) + 1.0), 1)

        def s_ln(h, v):
            c, rstd = normed(v["z"])
            gain, target = gain_ref[h], cur[h][2]
            rate = jnp.where(low1, cur[h][5], 0.0) if even else jnp.where(low1, 0.0, cur[h][5])
            v["c"], v["rstd"] = c, rstd
            g2c = gain * gain * c
            m2 = jnp.mean(g2c, 0, keepdims=True)
            m3 = jnp.mean(g2c * c, 0, keepdims=True)
            m4 = jnp.mean(target * c, 0, keepdims=True)
            e = rstd * rstd * (rstd * m3 + m4)
            v["dz"] = rstd * rate * ((g2c - m2) * rstd + target - c * e)

        def s_t(h, v):
            v["dzt"] = jnp.concatenate([jnp.transpose(jnp.concatenate([x, x], 0))[sl] for x in split(v["dz"])], 1)

        def s_da(h, v):
            v["da"] = dot(v["dzt"], stack4(*v["w2"], 0))

        def s_dh(h, v):
            v["dh"] = v["da"] * v["slope"]
            live["dh"][h] = jnp.concatenate(split(v["dh"]), 0)

        def s_dw2(h, v):
            d = v["dz"] + pltpu.roll(v["dz"], 64, 1)
            dw2 = dot(jnp.concatenate(split(d), 1), stack4(v["act"][0][sl], v["act"][1][sl], 0))
            live["w2"][h] = live["w2"][h] - 0.25 * dw2
            live["c2"][h] = live["c2"][h] - jnp.sum(v["dz"], 1, keepdims=True)

        def s_state(h, v):
            live["w1"][h] = v["w1"]
            live["c1"][h] = v["c1"] - jnp.sum(v["dh"], 0, keepdims=True)

        def s_y(h, v):
            q = last[h][1] if even else cur[h][1]
            v["y"] = v["c"] * v["rstd"] * gain_ref[h] + (q + shift_ref[h])

        def s_prep(h, v):
            if even:
                nxt[h] = prep(b, tile, h)

        stages = dict(upd=s_upd, gelu=s_gelu, w2=s_w2, z=s_z, w1=s_w1, x=s_x, base=s_base, corr=s_corr, ln=s_ln,
                      t=s_t, da=s_da, dh=s_dh, dw2=s_dw2, state=s_state, y=s_y, prep=s_prep)
        order = sorted((at + SKEW * h, i, h, name) for i, (name, at) in enumerate(ORDER) for h in heads)
        for _, _, h, name in order:
            stages[name](h, vs[h])
        return [v["y"] for v in vs]

    def put(b, tile, first, then):
        for h in heads:
            out_ref[b, h * 64:h * 64 + 64, tile * 128:tile * 128 + 128] = jnp.where(low, first[h], then[h]).astype(bf16)

    def save(cur, last):
        for h in heads:
            xk_ref[h], xq_ref[h], xt_ref[h] = cur[h][0], cur[h][1], cur[h][2]
            xd_ref[0, h], xd_ref[1, h], xd_ref[2, h] = cur[h][3], cur[h][4], last[h][4]
            rate_ref[h], xq_ref[nh + h] = cur[h][5], last[h][1]

    def block(b, _):
        load()
        cur = [(xk_ref[h], xq_ref[h], xt_ref[h], xd_ref[0, h], xd_ref[1, h], rate_ref[h]) for h in heads]
        last = [(None, xq_ref[nh + h], None, None, xd_ref[2, h], None) for h in heads]
        mid, end = [None] * nh, [None] * nh
        y = step(b, 1, True, cur, last, mid)
        put(jnp.maximum(b - 1, 0), 1, [yprev_ref[h] for h in heads], y)
        first = step(b, 1, False, cur, last, mid)
        then = step(jnp.minimum(b + 1, nb - 1), 0, True, mid, cur, end)
        put(b, 0, first, then)
        y = step(b, 0, False, mid, cur, end)
        for h in heads:
            yprev_ref[h] = y[h]
        save(end, mid)
        store()
        return 0

    first = [prep(0, 0, h) for h in heads]
    for h in heads:
        xs = jnp.concatenate(tokmajor(first[h][0]), 1)
        base_ref[h] = dot(xs, stack4(*split(w1_ref[h]), 0)) + c1_ref[h]
    save(first, [(None, jnp.zeros((64, 128), f32), None, None, jnp.zeros((64, 256), bf16), None)] * nh)
    lax.fori_loop(0, nb, block, 0, unroll=UNROLL)
    load()
    y = []
    for h in heads:
        hid, _ = hidden(h, xd_ref[2, h])
        c, rstd = normed(second(h, gelu(hid, None)[0], split(live["w2"][h])))
        y.append(c * rstd * gain_ref[h] + (xq_ref[nh + h] + shift_ref[h]))
    put(nb - 1, 1, [yprev_ref[h] for h in heads], y)


def ttt(x, cos, sin, gain, shift, own):
    nh = gain.shape[0]
    return pl.pallas_call(
        ttt_kernel,
        out_shape=jax.ShapeDtypeStruct((x.shape[0], nh * 64, x.shape[2]), bf16),
        in_specs=[pl.BlockSpec(memory_space=pltpu.VMEM)] * 6,
        out_specs=pl.BlockSpec(memory_space=pltpu.VMEM),
        scratch_shapes=[
            pltpu.VMEM((nh, 64, 256), f32),
            pltpu.VMEM((nh, 1, 256), f32),
            pltpu.VMEM((nh, 64, 256), f32),
            pltpu.VMEM((nh, 64, 128), f32),
            pltpu.VMEM((nh, 64, 128), f32),
            pltpu.VMEM((nh, 128, 256), f32),
            pltpu.VMEM((nh, 128, 256), bf16),
            pltpu.VMEM((nh, 128, 256), bf16),
            pltpu.VMEM((nh, 64, 128), f32),
            pltpu.VMEM((2 * nh, 64, 128), f32),
            pltpu.VMEM((nh, 64, 128), f32),
            pltpu.VMEM((3, nh, 64, 256), bf16),
            pltpu.VMEM((nh, 1, 128), f32),
        ],
        compiler_params=pltpu.CompilerParams(vmem_limit_bytes=48 * 1024 * 1024),
    )(x, cos, sin, gain, shift, own)


def pack_kernel(w1_ref, c1_ref, w2_ref, c2_ref, out_ref):
    nh = w1_ref.shape[1]
    c1 = jnp.concatenate([c1_ref[h] for h in range(nh)], 0)
    for h in range(nh):
        hl = slice(h * 256, h * 256 + 256)
        for i in range(8):
            out_ref[i, :, hl] = w1_ref[0, h, i * 8:i * 8 + 8]
            out_ref[8 + i, :, hl] = w2_ref[0, h, i * 8:i * 8 + 8]
    out_ref[:, :, nh * 256:] = jnp.zeros_like(out_ref[:, :, nh * 256:])
    for i in range(16):
        out_ref[i, :nh, nh * 256:] = c1[:, :128]
        out_ref[i, nh:2 * nh, nh * 256:] = c1[:, 128:]
        for h in range(nh):
            at = nh * 256 + h % 2 * 64
            out_ref[i, 2 * nh + h // 2:2 * nh + h // 2 + 1, at:at + 64] = c2_ref[h]


def pack(w1, c1, w2, c2):
    return pl.pallas_call(
        pack_kernel,
        out_shape=jax.ShapeDtypeStruct((16, 8, w1.shape[1] * 256 + 128), f32),
        in_specs=[pl.BlockSpec(memory_space=pltpu.VMEM)] * 4,
        out_specs=pl.BlockSpec(memory_space=pltpu.VMEM),
        compiler_params=pltpu.CompilerParams(vmem_limit_bytes=48 * 1024 * 1024),
    )(w1, c1, w2, c2)


def tables(off, n):
    half = 32
    freqs = jnp.exp(-jnp.log(10000.0) * jnp.arange(half, dtype=f32) / half)
    pos = (off + jnp.arange(n, dtype=jnp.int32)).astype(f32)
    ang = pos.reshape(n // 256, 1, 256) * freqs[None, :, None]
    return jnp.cos(ang), jnp.sin(ang)


def body(
    query_proj,
    key_proj,
    value_proj,
    learn_rate,
    norm_gain,
    norm_shift,
    start_offset,
    owner_map,
    first_weight,
    first_bias,
    second_weight,
    second_bias,
):
    groups = lax.axis_size("seq")
    nh, tok = first_weight.shape[1], query_proj.shape[1]

    packed = pack(first_weight, jnp.swapaxes(first_bias, 0, 1), jnp.swapaxes(second_weight, 2, 3), jnp.swapaxes(second_bias, 0, 1))
    held = lax.all_to_all(packed, "branch", split_axis=0, concat_axis=0, tiled=True)
    picked = held.at[owner_map].get(mode="promise_in_bounds")
    own = lax.all_to_all(picked, "branch", split_axis=0, concat_axis=0, tiled=True)

    def column(x):
        return jnp.broadcast_to(x[:, :, None], x.shape + (128,))

    def by_group(x):
        return x[0].T.reshape(groups, x.shape[2] // groups, tok)

    rates = jnp.pad(by_group(learn_rate), ((0, 0), (0, 16 - nh), (0, 0)))
    x = jnp.concatenate([by_group(query_proj), by_group(key_proj), by_group(value_proj), rates], 1)
    x = lax.all_to_all(x, "seq", split_axis=0, concat_axis=0, tiled=True)
    cos, sin = tables(start_offset[0], groups * tok)
    y = ttt(x, cos, sin, column(norm_gain), column(norm_shift), own)
    y = lax.all_to_all(y, "seq", split_axis=0, concat_axis=0, tiled=True)
    return y.reshape(groups * nh * 64, tok).T[None]


def solution(mesh):
    return jax.shard_map(
        body,
        mesh=mesh,
        in_specs=(
            P("branch", "seq", None),
            P("branch", "seq", None),
            P("branch", "seq", None),
            P("branch", "seq", None),
            P("seq", None),
            P("seq", None),
            P("branch"),
            P(),
            P("branch", "seq", None, None),
            P("branch", "seq", None),
            P("branch", "seq", None, None),
            P("branch", "seq", None),
        ),
        out_specs=P("branch", "seq", None),
        check_vma=False,
    )
```
